32 devices in a mesh: row: 4 (over z), col: 8 (over y, x, core).
Axes of the slice: x: 2, y: 2, z: 4, core: 2. Of those that a mesh axis runs over, the one named last changes fastest.
Arguments:
- lower_vectors: bfloat16 [192, 65536], P('col', 'row'), may hold values from -0.0234375 to 0.0234375
- upper_vectors: bfloat16 [1024, 65536], P('col', 'row'), may hold values from -0.0234375 to 0.0234375
- vib_dipole: bfloat16 [3, 256, 256], replicated, may hold values from -96 to 96
- rot_factor: float32 [3, 256], P(None, 'row'), may hold values from 0.5 to 1.5
- population: float32 [192], P('row'), may hold values from 0.02 to 0.4
- broadening: float32 [192], P('row'), may hold values from 0.5 to 2
- lower_symmetry: int32 [192], P('row'), may hold values from 0 to 7
- upper_symmetry: int32 [1024], P('col'), may hold values from 0 to 7
- symmetry_pairs: int32 [8], replicated, may hold values from 0 to 7, each once
- width_class: int32 [192, 1024], P('row', 'col'), may hold values from 0 to 7
- width_table: float32 [8], replicated, may hold values from 0.5 to 6
- line_shard: int32 [192, 1024], P('row', 'col'), may hold values from 0 to 31, as said below
- line_bin: int32 [192, 1024], P('row', 'col'), may hold values from 0 to 8191
- bin_offset: float32 [192, 1024], P('row', 'col'), may hold values from 0 to 1
Outputs:
- amplitudes: float32 [192, 1024], P('row', 'col')
- spectrum: float32 [262144], P(('row', 'col'))
The draws below stay inside these ranges and needn't reach their ends.
Inputs may be any that keep to these rules, and one draw needn't show every extreme that they name: `line_shard`: for each device's block of lines (48 lower by 128 upper states), exactly 768 lines name one grid shard that is common to all devices and drawn from the seed; each other shard is named by the block's lines an equal number of times up to one.
All inputs are finite; a program needn't handle non-finite values.
Results may differ from the reference program's by a relative error of at most 0.0029.
Values may be sent and summed in bfloat16 or wider, within the bound.
A program may use at most 128 MiB of HBM per device.

```python
import math
import jax
import jax.numpy as jnp
from jax import lax

NK = 256
NV = 256
HW = 64
NCLASS = 8
NSYM = 8
UPPER_DEV = 128
GRID_DEV = 8192
B = 65536
NL = 192
NU = 1024
LOW_ROWS = 48
CAP = 768
GRID = 262144
N_ROW = 4
N_COL = 8
DEVICES = 32


def draw_line_shard(key, part):
    key = jax.random.fold_in(key, 11)
    hot_key, order_key, base_key = jax.random.split(key, 3)
    hot_shard = jax.random.randint(hot_key, (), 0, DEVICES)
    line_count = LOW_ROWS * UPPER_DEV
    block_keys = jax.random.split(order_key, DEVICES)
    ranks = jax.vmap(lambda block_key: jax.random.permutation(block_key, line_count))(block_keys)
    base_shift = jax.random.randint(base_key, (), 0, DEVICES - 1)
    block_ids = jnp.arange(DEVICES, dtype=jnp.int32)
    block_shift = (base_shift + block_ids * ((line_count - CAP) % (DEVICES - 1))) % (DEVICES - 1)
    others = (ranks - CAP + block_shift[:, None]) % (DEVICES - 1)
    others = others + (others >= hot_shard).astype(jnp.int32)
    owners = jnp.where(ranks < CAP, hot_shard, others)
    owners = owners.reshape(N_ROW, N_COL, LOW_ROWS, UPPER_DEV).transpose(0, 2, 1, 3).reshape(NL, NU)
    return owners.astype(jnp.int32)


def draw_line_bin(key, part):
    key = jax.random.fold_in(key, 23)
    spread_key, edge_key, side_key = jax.random.split(key, 3)
    spread = jax.random.randint(spread_key, (NL, NU), 0, GRID_DEV)
    near = jax.random.randint(edge_key, (NL, NU), 0, max(HW // 2, 1))
    side = jax.random.randint(side_key, (NL, NU), 0, 4)
    bins = jnp.where(side == 0, GRID_DEV - 1 - near, jnp.where(side == 1, near, spread))
    bins = bins.at[0, 0].set(0).at[0, 1].set(GRID_DEV - 1)
    return bins.astype(jnp.int32)


def with_ends(values, key, smallest, top_value):
    dims = values.shape
    place = [jax.random.randint(jax.random.fold_in(key, axis), (), 0, dims[axis]) for axis in range(len(dims))]
    values = values.at[tuple(place)].set(smallest)
    longest = dims.index(max(dims))
    place[longest] = (place[longest] + 1) % dims[longest]
    return values.at[tuple(place)].set(top_value)


def block_scale(own_key, dims, cuts, low, top_value):
    gain, own = 1.0, jax.random.fold_in(own_key, 6)
    for dim, parts in cuts:
        heights = jnp.exp(jax.random.uniform(jax.random.fold_in(own, dim), (parts,), jnp.float32, low / len(cuts), top_value / len(cuts)))
        gain = gain * jnp.repeat(heights, dims[dim] // parts).reshape([-1 if axis == dim else 1 for axis in range(len(dims))])
    return gain


def noise(key, dims, deviation, bound, shards=(), kind=jnp.bfloat16):
    entries = jax.random.normal(key, dims, jnp.float32) * deviation
    if len(shards) > 0:
        entries = block_scale(key, dims, shards, -0.22, 0.18) * entries
    return jnp.clip(entries, min=-bound, max=bound).astype(kind)


def setup_inputs(seed: int = 0) -> dict:
    keys = jax.random.split(jax.random.key(seed), 15)
    lower_vectors = noise(keys[0], (NL, B), B ** -0.5, 0.0234375, ((0, 8), (1, 4)))
    upper_vectors = noise(keys[1], (NU, B), B ** -0.5, 0.0234375, ((0, 8), (1, 4)))
    vib_dipole = noise(keys[2], (3, NV, NV), (NK ** 0.5), 96.0)
    rot_factor = jnp.clip(0.5 + 1.0 * jax.random.uniform(keys[3], (3, NK), jnp.float32) ** block_scale(keys[3], (3, NK), ((1, 4),), -0.2, 0.2), 0.5, 1.5)
    population = jnp.clip(jnp.exp(math.log(0.4) - 2.9957323 * jax.random.uniform(keys[4], (NL,), jnp.float32) ** block_scale(keys[4], (NL,), ((0, 4),), -0.2, 0.2)), 0.02, 0.4)
    broadening = jnp.clip(jnp.exp(math.log(2.0) - 1.3862944 * jax.random.uniform(keys[5], (NL,), jnp.float32) ** block_scale(keys[5], (NL,), ((0, 4),), -0.2, 0.2)), 0.5, 2.0)
    lower_symmetry = with_ends(jax.random.randint(keys[6], (NL,), 0, NSYM), jax.random.fold_in(keys[6], 1), 0, NSYM - 1).astype(jnp.int32)
    upper_symmetry = with_ends(jax.random.randint(keys[7], (NU,), 0, NSYM), jax.random.fold_in(keys[7], 1), 0, NSYM - 1).astype(jnp.int32)
    symmetry_pairs = jax.random.permutation(keys[8], NSYM).astype(jnp.int32)
    width_class = with_ends(jax.random.randint(keys[9], (NL, NU), 0, NCLASS), jax.random.fold_in(keys[9], 1), 0, NCLASS - 1).astype(jnp.int32)
    width_table = jnp.clip(jnp.exp(jax.random.uniform(keys[10], (NCLASS,), jnp.float32, math.log(0.5), math.log(6.0))), 0.5, 6.0)
    line_shard = draw_line_shard(jax.random.fold_in(keys[14], 71), 0)
    line_bin = draw_line_bin(jax.random.fold_in(keys[14], 71), 0)
    bin_offset = jnp.clip(1.0 * jax.random.uniform(keys[13], (NL, NU), jnp.float32) ** block_scale(keys[13], (NL, NU), ((0, 4), (1, 8)), -0.2, 0.2), 0.0, 1.0)
    return {"lower_vectors": lower_vectors, "upper_vectors": upper_vectors, "vib_dipole": vib_dipole, "rot_factor": rot_factor, "population": population, "broadening": broadening, "lower_symmetry": lower_symmetry, "upper_symmetry": upper_symmetry, "symmetry_pairs": symmetry_pairs, "width_class": width_class, "width_table": width_table, "line_shard": line_shard, "line_bin": line_bin, "bin_offset": bin_offset}


doppler_base = 1.5
log_two = math.log(2.0)

def line_profile(strength, offset, lorentz, center, grid_total):
    step_grid = jnp.arange(2 * HW).astype(jnp.float32) - HW
    distance = step_grid[None, :] - offset[:, None]
    square = distance * distance
    doppler = doppler_base * (1.0 + center / grid_total)
    gauss_part = math.sqrt(log_two / math.pi) / doppler[:, None] * jnp.exp(-log_two * square / (doppler * doppler)[:, None])
    lorentz_part = lorentz[:, None] / (math.pi * (square + (lorentz * lorentz)[:, None]))
    mixing = lorentz / (lorentz + doppler)
    profile = mixing[:, None] * lorentz_part + (1.0 - mixing)[:, None] * gauss_part
    return strength[:, None] * profile

def reference(lower_vectors, upper_vectors, vib_dipole, rot_factor, population, broadening, lower_symmetry, upper_symmetry, symmetry_pairs, width_class, width_table, line_shard, line_bin, bin_offset):
    upper_blocks = upper_vectors.reshape(N_COL, UPPER_DEV, NK, NV)
    dipole_f = vib_dipole.astype(jnp.float32)

    def weigh_block(block_rows):
        padded = jnp.pad(block_rows.astype(jnp.float32), ((0, 0), (1, 1), (0, 0)))
        summed = jnp.zeros((UPPER_DEV, NK, NV), jnp.float32)
        for band_index in range(3):
            shifted = padded[:, band_index:band_index + NK, :]
            product_band = jnp.einsum('ukj,ij->uki', shifted, dipole_f[band_index])
            summed = summed + rot_factor[band_index][None, :, None] * product_band
        return summed.astype(jnp.bfloat16)
    weighted = lax.map(weigh_block, upper_blocks).reshape(NU, B)
    amplitudes = jnp.dot(lower_vectors.astype(jnp.float32), weighted.astype(jnp.float32).T, preferred_element_type=jnp.float32)
    allowed = symmetry_pairs[lower_symmetry]
    keep_mask = (upper_symmetry[None, :] == allowed[:, None]).astype(jnp.float32)
    strength = population[:, None] * amplitudes * amplitudes * keep_mask
    lorentz = width_table[width_class] * broadening[:, None]
    grid_total = float(GRID)
    full_grid = jnp.zeros((GRID + 2 * HW,), jnp.float32)

    def add_rows(block_index, buffer):
        first_row = (block_index * 8).astype(jnp.int32)

        def window_of(array):
            return lax.dynamic_slice_in_dim(array, first_row, 8, 0).reshape(-1)
        position = window_of(line_shard) * GRID_DEV + window_of(line_bin)
        offset = window_of(bin_offset)
        center = position.astype(jnp.float32) + offset
        contribution = line_profile(window_of(strength), offset, window_of(lorentz), center, grid_total)
        targets = position[:, None] + jnp.arange(2 * HW).astype(jnp.int32)[None, :]
        return buffer.at[targets].add(contribution)
    full_grid = lax.fori_loop(0, NL // 8, add_rows, full_grid)
    spectrum = full_grid[HW:HW + GRID]
    return (amplitudes, spectrum)
```

```python
import functools
import math

import jax
import jax.numpy as jnp
from jax import lax
from jax.experimental import pallas as pl
from jax.experimental.pallas import tpu as pltpu
from jax.sharding import PartitionSpec as P

NV = 256
HW = 64
GRID_DEV = 8192
LANE = 128
TILES_DEV = GRID_DEV // LANE
GROUP = 4
MESH = pl.DeviceIdType.MESH

doppler_base = 1.5
log_two = math.log(2.0)

f32 = jnp.float32
bf16 = jnp.bfloat16


def flip(index, mask):
    bit = 1
    while bit <= mask:
        if mask & bit:
            index = index + bit - 2 * bit * ((index // bit) % 2)
        bit *= 2
    return index


def iota(shape, dim):
    return lax.broadcasted_iota(jnp.int32, shape, dim)


def column_of(row_value):
    n = row_value.shape[1]
    eye = iota((n, n), 0) == iota((n, n), 1)
    return jnp.sum(jnp.where(eye, row_value, jnp.zeros_like(row_value)), axis=1, keepdims=True)


def kernel(
    nrow,
    ncol,
    lower_ref,
    upper_ref,
    vib_ref,
    rot_ref,
    population_ref,
    broadening_ref,
    lower_sym_ref,
    upper_sym_ref,
    pairs_ref,
    width_class_ref,
    table_ref,
    shard_ref,
    bin_ref,
    offset_ref,
    amp_ref,
    spec_ref,
    padded,
    weighted,
    gathered,
    partial,
    amp_in,
    coef,
    place,
    unit,
    windows,
    onehot,
    outgoing,
    incoming,
    totals,
    arrived,
    local_sem,
    halo_send,
    halo_recv,
    gather_send,
    gather_recv,
    amp_send,
    amp_recv,
    col_send,
    col_recv,
    row_send,
    row_recv,
):
    row = lax.axis_index("row")
    col = lax.axis_index("col")
    uppers, basis = upper_ref.shape
    slabs = basis // NV
    two, pair_rows, piece = lower_ref.shape
    lows = pair_rows // 2
    low_rows, lines = bin_ref.shape
    tiles = nrow * ncol * TILES_DEV
    chunk = ncol * TILES_DEV
    bits = []
    bit = ncol // 2
    while bit:
        bits.append(bit)
        bit //= 2
    orders = [bits, [bits[1], bits[0]] + bits[2:]]

    load = pltpu.make_async_copy(upper_ref, padded.at[:, pl.ds(NV, basis)], local_sem.at[0])
    load.start()
    own = pltpu.make_async_copy(lower_ref, gathered.at[:, pl.ds(0, pair_rows)], local_sem.at[1])
    own.start()

    barrier = pltpu.get_barrier_semaphore()
    for d in range(1, ncol):
        pl.semaphore_signal(
            barrier, inc=1, device_id=(row, (col + d) % ncol), device_id_type=MESH
        )
    for d in range(1, nrow):
        pl.semaphore_signal(
            barrier, inc=1, device_id=((row + d) % nrow, col), device_id_type=MESH
        )
    pl.semaphore_wait(barrier, ncol + nrow - 2)

    def piece_copy(half, mask, bit):
        if mask == 0:
            src = lower_ref.at[half]
        else:
            src = gathered.at[half, pl.ds(mask * pair_rows, pair_rows)]
        to = mask ^ bit
        return pltpu.make_async_remote_copy(
            src_ref=src,
            dst_ref=gathered.at[half, pl.ds(to * pair_rows, pair_rows)],
            send_sem=gather_send.at[half, to],
            recv_sem=gather_recv.at[half, to],
            device_id=(row, flip(col, bit)),
            device_id_type=MESH,
        )

    up = pltpu.make_async_remote_copy(
        src_ref=upper_ref.at[:, pl.ds(basis - NV, NV)],
        dst_ref=padded.at[:, pl.ds(0, NV)],
        send_sem=halo_send.at[0],
        recv_sem=halo_recv.at[0],
        device_id=((row + 1) % nrow, col),
        device_id_type=MESH,
    )
    down = pltpu.make_async_remote_copy(
        src_ref=upper_ref.at[:, pl.ds(0, NV)],
        dst_ref=padded.at[:, pl.ds(basis + NV, NV)],
        send_sem=halo_send.at[1],
        recv_sem=halo_recv.at[1],
        device_id=((row + nrow - 1) % nrow, col),
        device_id_type=MESH,
    )
    pl.when(row < nrow - 1)(lambda: up.start())
    pl.when(row > 0)(lambda: down.start())

    started = []

    def send(half, mask, bit):
        copy = piece_copy(half, mask, bit)
        copy.start()
        started.append(copy)

    for level in range(len(bits)):
        for half in range(2):
            send(half, 0, orders[half][level])

    broad = column_of(broadening_ref[...])
    width_class = width_class_ref[...]
    lorentz = jnp.zeros(width_class.shape, f32)
    for i in range(table_ref.shape[0]):
        lorentz = lorentz + jnp.where(width_class == i, table_ref[i], 0.0)
    lorentz = lorentz * broad
    position = shard_ref[...] * GRID_DEV + bin_ref[...]
    center = position.astype(f32) + offset_ref[...]
    doppler = doppler_base * (1.0 + center / float(GRID_DEV * nrow * ncol))
    mixing = lorentz / (lorentz + doppler)
    coef[0] = mixing * lorentz / math.pi
    coef[1] = lorentz * lorentz
    coef[2] = (1.0 - mixing) * (math.sqrt(log_two / math.pi) / doppler)
    coef[3] = -log_two / (doppler * doppler)
    coef[4] = offset_ref[...]
    start = position - HW
    place[0] = lax.shift_right_arithmetic(start, 7)
    place[1] = lax.bitwise_and(start, LANE - 1)

    load.wait()

    @pl.when(row == 0)
    def _():
        padded[:, pl.ds(0, NV)] = jnp.zeros((uppers, NV), bf16)

    @pl.when(row == nrow - 1)
    def _():
        padded[:, pl.ds(basis + NV, NV)] = jnp.zeros((uppers, NV), bf16)

    pl.when(row > 0)(lambda: up.wait_recv())
    pl.when(row < nrow - 1)(lambda: down.wait_recv())

    half_slabs = slabs // 2

    def weigh(g, _):
        first = g * GROUP
        sums = [jnp.zeros((uppers, NV), f32) for _ in range(GROUP)]
        for band in range(3):
            blocks = [
                padded[:, pl.ds(pl.multiple_of((first + j + band) * NV, NV), NV)]
                for j in range(GROUP)
            ]
            product = lax.dot_general(
                jnp.concatenate(blocks, axis=0),
                vib_ref[band],
                (((1,), (1,)), ((), ())),
                preferred_element_type=f32,
            )
            for j in range(GROUP):
                sums[j] = sums[j] + rot_ref[band, first + j] * product[j * uppers : (j + 1) * uppers]
        part = first // half_slabs
        for j in range(GROUP):
            at = pl.multiple_of((first + j - part * half_slabs) * NV, NV)
            weighted[pl.ds(pl.multiple_of(part * uppers, uppers), uppers), pl.ds(at, NV)] = sums[
                j
            ].astype(bf16)
        return 0

    lax.fori_loop(0, slabs // GROUP, weigh, 0)

    def slots_of(half, level):
        order = orders[half]
        masks = [0]
        for b in order[:level]:
            masks = masks + [m ^ b for m in masks]
        return [(m, m ^ order[level]) for m in masks]

    def forward(level):
        count = len(slots_of(0, level))
        for i in range(count):
            for half in range(2):
                mask, slot = slots_of(half, level)[i]
                piece_copy(half, mask, orders[half][level]).wait_recv()
                for later in orders[half][level + 1 :]:
                    send(half, slot, later)

    forward(0)

    cell = iota((LANE, lines), 0)

    def shape_row(r, _):
        inside = place[1, pl.ds(r, 1), :]
        step = lax.bitwise_and(cell - inside, LANE - 1) - HW
        x = step.astype(f32) - coef[4, pl.ds(r, 1), :]
        square = x * x
        unit[r] = coef[0, pl.ds(r, 1), :] / (square + coef[1, pl.ds(r, 1), :]) + coef[
            2, pl.ds(r, 1), :
        ] * jnp.exp(coef[3, pl.ds(r, 1), :] * square)
        return 0

    lax.fori_loop(0, low_rows, shape_row, 0)

    tile_iota = iota((chunk, lines), 0)

    def build(m, slot):
        def build_row(r, _):
            tile = place[0, pl.ds(r, 1), :]
            tile = jnp.where(tile < 0, tile + tiles, tile) - m * chunk
            hit = jnp.where(tile_iota == tile, 1.0, 0.0).astype(bf16)
            onehot[slot, :, pl.ds(pl.multiple_of(r * lines, lines), lines)] = hit
            return 0

        lax.fori_loop(0, low_rows, build_row, 0)

    early = onehot.shape[0] == nrow
    split = nrow // 2
    if early:
        lax.fori_loop(0, split, lambda m, _: (build(m, m), 0)[1], 0)
    for level in range(1, len(bits) - 1):
        forward(level)
    if early:
        lax.fori_loop(split, nrow, lambda m, _: (build(m, m), 0)[1], 0)
    forward(len(bits) - 1)
    own.wait()

    total = jnp.zeros((ncol * pair_rows, 2 * uppers), f32)
    for half in range(2):
        total = total + lax.dot_general(
            gathered[half],
            weighted[:, pl.ds(half * piece, piece)],
            (((1,), (1,)), ((), ())),
            preferred_element_type=f32,
        )
    for mask in range(ncol):
        base = mask * pair_rows
        rows = total[base : base + lows, :uppers] + total[base + lows : base + 2 * lows, uppers:]
        partial[pl.ds(pl.multiple_of(flip(col, mask) * lows, 8), lows), :] = rows

    def amp_rows(owner):
        return partial.at[pl.ds(pl.multiple_of(owner * low_rows, 8), low_rows)]

    amp_copies = []
    for d in range(1, nrow):
        to = (row + d) % nrow
        copy = pltpu.make_async_remote_copy(
            src_ref=amp_rows(to),
            dst_ref=amp_in.at[d - 1],
            send_sem=amp_send.at[d - 1],
            recv_sem=amp_recv.at[d - 1],
            device_id=(to, col),
            device_id_type=MESH,
        )
        copy.start()
        amp_copies.append(copy)
    population = column_of(population_ref[...])
    lower_sym = lower_sym_ref[...]
    allowed = jnp.zeros(lower_sym.shape, jnp.int32)
    for i in range(pairs_ref.shape[0]):
        allowed = allowed + jnp.where(lower_sym == i, pairs_ref[i], 0)
    allowed = column_of(allowed)
    keep = jnp.where(upper_sym_ref[...] == allowed, 1.0, 0.0)
    amplitudes = partial[pl.ds(pl.multiple_of(row * low_rows, 8), low_rows), :]
    for d in range(1, nrow):
        amp_copies[d - 1].wait_recv()
        amplitudes = amplitudes + amp_in[d - 1]
    amp_ref[...] = amplitudes
    coef[5] = population * amplitudes * amplitudes * keep

    def scale_row(r, before):
        inside = place[1, pl.ds(r, 1), :]
        tile = place[0, pl.ds(r, 1), :]
        value = unit[r] * coef[5, pl.ds(r, 1), :]
        is_head = cell >= inside
        head = jnp.where(is_head & (tile >= 0), value, 0.0)
        tail = jnp.where(is_head | (tile >= tiles - 1), 0.0, value)
        lane = pl.ds(pl.multiple_of(r * lines, lines), lines)
        windows[pl.ds(0, LANE), lane] = head.astype(bf16)
        windows[pl.ds(LANE, LANE), lane] = tail.astype(bf16)
        return before + jnp.where(tile < 0, tail, 0.0)

    before = lax.fori_loop(0, low_rows, scale_row, jnp.zeros((LANE, lines), f32))
    before = jnp.sum(before, axis=1, keepdims=True)
    eye = iota((LANE, LANE), 0) == iota((LANE, LANE), 1)
    carry = jnp.sum(jnp.where(eye, before, 0.0), axis=0, keepdims=True)
    first_row = iota((chunk, LANE), 0) == 0

    def col_copy(d, m):
        to = (col + d) % ncol
        return pltpu.make_async_remote_copy(
            src_ref=outgoing.at[m, to],
            dst_ref=incoming.at[m, d - 1],
            send_sem=col_send.at[m, d - 1],
            recv_sem=col_recv.at[m, d - 1],
            device_id=(row, to),
            device_id_type=MESH,
        )

    def bin_chunk(m, carry):
        if not early:
            build(m, 0)
        slot = m if early else 0
        product = lax.dot_general(
            onehot[slot], windows[...], (((1,), (1,)), ((), ())), preferred_element_type=f32
        )
        tail = product[:, LANE:]
        shifted = jnp.where(first_row, carry, pltpu.roll(tail, 1, 0))
        cells = product[:, :LANE] + shifted
        outgoing[m] = cells.astype(bf16).reshape(ncol, TILES_DEV, LANE)
        for d in range(1, ncol):
            col_copy(d, m).start()
        return tail[chunk - 1 :, :]

    lax.fori_loop(0, nrow, bin_chunk, carry)

    def add_chunk(m, _):
        value = outgoing[m, col].astype(f32)
        for d in range(1, ncol):
            col_copy(d, m).wait_recv()
            value = value + incoming[m, d - 1].astype(f32)
        totals[m] = value
        return 0

    lax.fori_loop(0, nrow, add_chunk, 0)
    row_copies = []
    for d in range(1, nrow):
        to = (row + d) % nrow
        copy = pltpu.make_async_remote_copy(
            src_ref=totals.at[to],
            dst_ref=arrived.at[d - 1],
            send_sem=row_send.at[d - 1],
            recv_sem=row_recv.at[d - 1],
            device_id=(to, col),
            device_id_type=MESH,
        )
        copy.start()
        row_copies.append(copy)
    value = totals[row]
    for d in range(1, nrow):
        row_copies[d - 1].wait_recv()
        value = value + arrived[d - 1]
    spec_ref[...] = value

    for copy in started + amp_copies + row_copies:
        copy.wait_send()

    def drain(m, _):
        for d in range(1, ncol):
            col_copy(d, m).wait_send()
        return 0

    lax.fori_loop(0, nrow, drain, 0)
    pl.when(row < nrow - 1)(lambda: up.wait_send())
    pl.when(row > 0)(lambda: down.wait_send())


def shards(
    lower_vectors,
    upper_vectors,
    vib_dipole,
    rot_factor,
    population,
    broadening,
    lower_symmetry,
    upper_symmetry,
    symmetry_pairs,
    width_class,
    width_table,
    line_shard,
    line_bin,
    bin_offset,
):
    nrow, ncol = lax.axis_size("row"), lax.axis_size("col")
    lows, basis = lower_vectors.shape
    uppers = upper_vectors.shape[0]
    low_rows, lines = line_bin.shape
    quarter = basis // 4
    pieces = lower_vectors.reshape(lows, 2, 2, quarter).transpose(2, 1, 0, 3)
    pieces = pieces.reshape(2, 2 * lows, quarter)
    chunk = ncol * TILES_DEV
    count = low_rows * lines
    early = nrow * chunk * count * 2 <= 26 * 2**20
    vmem = pl.BlockSpec(memory_space=pltpu.VMEM)
    smem = pl.BlockSpec(memory_space=pltpu.SMEM)
    hbm = pl.BlockSpec(memory_space=pl.ANY)
    dma = pltpu.SemaphoreType.DMA
    amplitudes, spectrum = pl.pallas_call(
        functools.partial(kernel, nrow, ncol),
        out_shape=(
            jax.ShapeDtypeStruct((low_rows, lines), f32),
            jax.ShapeDtypeStruct((TILES_DEV, LANE), f32),
        ),
        in_specs=[hbm, hbm, vmem, smem, vmem, vmem, vmem, vmem, smem, vmem, smem, vmem, vmem, vmem],
        out_specs=(vmem, vmem),
        scratch_shapes=[
            pltpu.VMEM((uppers, basis + 2 * NV), bf16),
            pltpu.VMEM((2 * uppers, basis // 2), bf16),
            pltpu.VMEM((2, ncol * 2 * lows, quarter), bf16),
            pltpu.VMEM((ncol * lows, uppers), f32),
            pltpu.VMEM((nrow - 1, low_rows, lines), f32),
            pltpu.VMEM((6, low_rows, lines), f32),
            pltpu.VMEM((2, low_rows, lines), jnp.int32),
            pltpu.VMEM((low_rows, LANE, lines), f32),
            pltpu.VMEM((2 * LANE, count), bf16),
            pltpu.VMEM((nrow if early else 1, chunk, count), bf16),
            pltpu.VMEM((nrow, ncol, TILES_DEV, LANE), bf16),
            pltpu.VMEM((nrow, ncol - 1, TILES_DEV, LANE), bf16),
            pltpu.VMEM((nrow, TILES_DEV, LANE), f32),
            pltpu.VMEM((nrow - 1, TILES_DEV, LANE), f32),
            dma((2,)),
            dma((2,)),
            dma((2,)),
            dma((2, ncol)),
            dma((2, ncol)),
            dma((nrow - 1,)),
            dma((nrow - 1,)),
            dma((nrow, ncol - 1)),
            dma((nrow, ncol - 1)),
            dma((nrow - 1,)),
            dma((nrow - 1,)),
        ],
        compiler_params=pltpu.CompilerParams(
            collective_id=0, has_side_effects=True, vmem_limit_bytes=58 * 2**20
        ),
    )(
        pieces,
        upper_vectors,
        vib_dipole,
        rot_factor,
        population[None, :],
        broadening[None, :],
        lower_symmetry[None, :],
        upper_symmetry[None, :],
        symmetry_pairs,
        width_class,
        width_table,
        line_shard,
        line_bin,
        bin_offset,
    )
    return (amplitudes, spectrum.reshape(GRID_DEV))


def solution(mesh):
    return jax.shard_map(
        shards,
        mesh=mesh,
        in_specs=(
            P("col", "row"),
            P("col", "row"),
            P(),
            P(None, "row"),
            P("row"),
            P("row"),
            P("row"),
            P("col"),
            P(),
            P("row", "col"),
            P(),
            P("row", "col"),
            P("row", "col"),
            P("row", "col"),
        ),
        out_specs=(P("row", "col"), P(("row", "col"))),
        check_vma=False,
    )
```

```python
import functools
import math

import jax
import jax.numpy as jnp
from jax import lax
from jax.experimental import pallas as pl
from jax.experimental.pallas import tpu as pltpu
from jax.sharding import PartitionSpec as P

NV = 256
HW = 64
GRID_DEV = 8192
LANE = 128
TILES_DEV = GRID_DEV // LANE
GROUP = 4
MESH = pl.DeviceIdType.MESH

doppler_base = 1.5
log_two = math.log(2.0)

f32 = jnp.float32
bf16 = jnp.bfloat16


def flip(index, mask):
    bit = 1
    while bit <= mask:
        if mask & bit:
            index = index + bit - 2 * bit * ((index // bit) % 2)
        bit *= 2
    return index


def iota(shape, dim):
    return lax.broadcasted_iota(jnp.int32, shape, dim)


def column_of(row_value):
    n = row_value.shape[1]
    eye = iota((n, n), 0) == iota((n, n), 1)
    return jnp.sum(jnp.where(eye, row_value, jnp.zeros_like(row_value)), axis=1, keepdims=True)


def kernel(
    nrow,
    ncol,
    lower_ref,
    upper_ref,
    vib_ref,
    rot_ref,
    population_ref,
    broadening_ref,
    lower_sym_ref,
    upper_sym_ref,
    pairs_ref,
    width_class_ref,
    table_ref,
    shard_ref,
    bin_ref,
    offset_ref,
    amp_ref,
    spec_ref,
    padded,
    weighted,
    gathered,
    partial,
    amp_in,
    coef,
    place,
    unit,
    windows,
    onehot,
    outgoing,
    incoming,
    totals,
    arrived,
    local_sem,
    halo_send,
    halo_recv,
    gather_send,
    gather_recv,
    amp_send,
    amp_recv,
    col_send,
    col_recv,
    row_send,
    row_recv,
):
    row = lax.axis_index("row")
    col = lax.axis_index("col")
    uppers, basis = upper_ref.shape
    slabs = basis // NV
    two, pair_rows, piece = lower_ref.shape
    lows = pair_rows // 2
    low_rows, lines = bin_ref.shape
    tiles = nrow * ncol * TILES_DEV
    chunk = ncol * TILES_DEV
    bits = []
    bit = ncol // 2
    while bit:
        bits.append(bit)
        bit //= 2
    orders = [bits, [bits[1], bits[0]] + bits[2:]]

    load = pltpu.make_async_copy(upper_ref, padded.at[:, pl.ds(NV, basis)], local_sem.at[0])
    load.start()
    own = pltpu.make_async_copy(lower_ref, gathered.at[:, pl.ds(0, pair_rows)], local_sem.at[1])
    own.start()

    barrier = pltpu.get_barrier_semaphore()
    for d in range(1, ncol):
        pl.semaphore_signal(
            barrier, inc=1, device_id=(row, (col + d) % ncol), device_id_type=MESH
        )
    for d in range(1, nrow):
        pl.semaphore_signal(
            barrier, inc=1, device_id=((row + d) % nrow, col), device_id_type=MESH
        )
    pl.semaphore_wait(barrier, ncol + nrow - 2)

    def slot_rows(mask):
        at = mask // 2 + (mask % 2) * (ncol // 2)
        return pl.ds(at * pair_rows, pair_rows)

    def piece_copy(half, mask, bit):
        if mask == 0:
            src = lower_ref.at[half]
        else:
            src = gathered.at[half, slot_rows(mask)]
        to = mask ^ bit
        return pltpu.make_async_remote_copy(
            src_ref=src,
            dst_ref=gathered.at[half, slot_rows(to)],
            send_sem=gather_send.at[half, to],
            recv_sem=gather_recv.at[half, to],
            device_id=(row, flip(col, bit)),
            device_id_type=MESH,
        )

    up = pltpu.make_async_remote_copy(
        src_ref=upper_ref.at[:, pl.ds(basis - NV, NV)],
        dst_ref=padded.at[:, pl.ds(0, NV)],
        send_sem=halo_send.at[0],
        recv_sem=halo_recv.at[0],
        device_id=((row + 1) % nrow, col),
        device_id_type=MESH,
    )
    down = pltpu.make_async_remote_copy(
        src_ref=upper_ref.at[:, pl.ds(0, NV)],
        dst_ref=padded.at[:, pl.ds(basis + NV, NV)],
        send_sem=halo_send.at[1],
        recv_sem=halo_recv.at[1],
        device_id=((row + nrow - 1) % nrow, col),
        device_id_type=MESH,
    )
    pl.when(row < nrow - 1)(lambda: up.start())
    pl.when(row > 0)(lambda: down.start())

    started = []

    def send(half, mask, bit):
        copy = piece_copy(half, mask, bit)
        copy.start()
        started.append(copy)

    for level in range(len(bits)):
        for half in range(2):
            send(half, 0, orders[half][level])

    broad = column_of(broadening_ref[...])
    width_class = width_class_ref[...]
    lorentz = jnp.zeros(width_class.shape, f32)
    for i in range(table_ref.shape[0]):
        lorentz = lorentz + jnp.where(width_class == i, table_ref[i], 0.0)
    lorentz = lorentz * broad
    position = shard_ref[...] * GRID_DEV + bin_ref[...]
    center = position.astype(f32) + offset_ref[...]
    doppler = doppler_base * (1.0 + center / float(GRID_DEV * nrow * ncol))
    mixing = lorentz / (lorentz + doppler)
    coef[0] = mixing * lorentz / math.pi
    coef[1] = lorentz * lorentz
    coef[2] = (1.0 - mixing) * (math.sqrt(log_two / math.pi) / doppler)
    coef[3] = -log_two / (doppler * doppler)
    coef[4] = offset_ref[...]
    start = position - HW
    place[0] = lax.shift_right_arithmetic(start, 7)
    place[1] = lax.bitwise_and(start, LANE - 1)

    cell = iota((LANE, lines), 0)

    def shape_row(r, _):
        inside = place[1, pl.ds(r, 1), :]
        step = lax.bitwise_and(cell - inside, LANE - 1) - HW
        x = step.astype(f32) - coef[4, pl.ds(r, 1), :]
        square = x * x
        unit[r] = coef[0, pl.ds(r, 1), :] / (square + coef[1, pl.ds(r, 1), :]) + coef[
            2, pl.ds(r, 1), :
        ] * jnp.exp(coef[3, pl.ds(r, 1), :] * square)
        return 0

    lax.fori_loop(0, low_rows, shape_row, 0)

    tile_iota = iota((chunk, lines), 0)

    def build(m, slot):
        def build_row(r, _):
            tile = place[0, pl.ds(r, 1), :]
            tile = jnp.where(tile < 0, tile + tiles, tile) - m * chunk
            hit = jnp.where(tile_iota == tile, 1.0, 0.0).astype(bf16)
            onehot[slot, :, pl.ds(pl.multiple_of(r * lines, lines), lines)] = hit
            return 0

        lax.fori_loop(0, low_rows, build_row, 0)

    early = onehot.shape[0] == nrow
    if early:
        lax.fori_loop(0, nrow, lambda m, _: (build(m, m), 0)[1], 0)

    load.wait()

    @pl.when(row == 0)
    def _():
        padded[:, pl.ds(0, NV)] = jnp.zeros((uppers, NV), bf16)

    @pl.when(row == nrow - 1)
    def _():
        padded[:, pl.ds(basis + NV, NV)] = jnp.zeros((uppers, NV), bf16)

    half_slabs = slabs // 2

    def weigh(g, _):
        first = g * GROUP
        sums = [jnp.zeros((uppers, NV), f32) for _ in range(GROUP)]
        for band in range(3):
            blocks = [
                padded[:, pl.ds(pl.multiple_of((first + j + band) * NV, NV), NV)]
                for j in range(GROUP)
            ]
            product = lax.dot_general(
                jnp.concatenate(blocks, axis=0),
                vib_ref[band],
                (((1,), (1,)), ((), ())),
                preferred_element_type=f32,
            )
            for j in range(GROUP):
                sums[j] = sums[j] + rot_ref[band, first + j] * product[j * uppers : (j + 1) * uppers]
        part = first // half_slabs
        for j in range(GROUP):
            at = pl.multiple_of((first + j - part * half_slabs) * NV, NV)
            weighted[pl.ds(pl.multiple_of(part * uppers, uppers), uppers), pl.ds(at, NV)] = sums[
                j
            ].astype(bf16)
        return 0

    def weigh_half(part):
        steps = half_slabs // GROUP
        lax.fori_loop(part * steps, (part + 1) * steps, weigh, 0)

    pl.when(row > 0)(lambda: up.wait_recv())
    weigh_half(0)

    def slots_of(half, level):
        order = orders[half]
        masks = [0]
        for b in order[:level]:
            masks = masks + [m ^ b for m in masks]
        return [(m, m ^ order[level]) for m in masks]

    def forward(level, begin=0, end=None):
        count = len(slots_of(0, level))
        for i in range(begin, count if end is None else end):
            for half in range(2):
                mask, slot = slots_of(half, level)[i]
                piece_copy(half, mask, orders[half][level]).wait_recv()
                for later in orders[half][level + 1 :]:
                    send(half, slot, later)

    forward(0)
    forward(1, 0, 1)
    pl.when(row < nrow - 1)(lambda: down.wait_recv())

    weigh_half(1)
    forward(1, 1)
    for level in range(2, len(bits) - 1):
        forward(level)
    own.wait()

    side = ncol // 2 * pair_rows
    amp_copies = []

    def sum_half(odd):
        total = jnp.zeros((side, 2 * uppers), f32)
        for half in range(2):
            total = total + lax.dot_general(
                gathered[half, pl.ds(odd * side, side)],
                weighted[:, pl.ds(half * piece, piece)],
                (((1,), (1,)), ((), ())),
                preferred_element_type=f32,
            )
        for i in range(ncol // 2):
            base = i * pair_rows
            rows = total[base : base + lows, :uppers] + total[base + lows : base + 2 * lows, uppers:]
            source = flip(col, 2 * i + odd)
            partial[pl.ds(pl.multiple_of(source * lows, 8), lows), :] = rows
        share = pl.multiple_of(flip(col % 2, odd) * lows, 8)
        for d in range(1, nrow):
            to = (row + d) % nrow
            copy = pltpu.make_async_remote_copy(
                src_ref=partial.at[pl.ds(pl.multiple_of(to * low_rows + share, 8), lows)],
                dst_ref=amp_in.at[d - 1, pl.ds(share, lows)],
                send_sem=amp_send.at[odd, d - 1],
                recv_sem=amp_recv.at[odd, d - 1],
                device_id=(to, col),
                device_id_type=MESH,
            )
            copy.start()
            amp_copies.append(copy)

    sum_half(0)
    forward(len(bits) - 1)
    sum_half(1)
    population = column_of(population_ref[...])
    lower_sym = lower_sym_ref[...]
    allowed = jnp.zeros(lower_sym.shape, jnp.int32)
    for i in range(pairs_ref.shape[0]):
        allowed = allowed + jnp.where(lower_sym == i, pairs_ref[i], 0)
    allowed = column_of(allowed)
    keep = jnp.where(upper_sym_ref[...] == allowed, 1.0, 0.0)
    amplitudes = partial[pl.ds(pl.multiple_of(row * low_rows, 8), low_rows), :]
    for copy in amp_copies:
        copy.wait_recv()
    for d in range(1, nrow):
        amplitudes = amplitudes + amp_in[d - 1]
    amp_ref[...] = amplitudes
    coef[5] = population * amplitudes * amplitudes * keep

    first_tile = ((row + 1) % nrow) * chunk

    def scale_row(r, before):
        inside = place[1, pl.ds(r, 1), :]
        tile = place[0, pl.ds(r, 1), :]
        value = unit[r] * coef[5, pl.ds(r, 1), :]
        is_head = cell >= inside
        head = jnp.where(is_head & (tile >= 0), value, 0.0)
        tail = jnp.where(is_head | (tile >= tiles - 1), 0.0, value)
        lane = pl.ds(pl.multiple_of(r * lines, lines), lines)
        windows[pl.ds(0, LANE), lane] = head.astype(bf16)
        windows[pl.ds(LANE, LANE), lane] = tail.astype(bf16)
        return before + jnp.where(tile == first_tile - 1, tail, 0.0)

    before = lax.fori_loop(0, low_rows, scale_row, jnp.zeros((LANE, lines), f32))
    before = jnp.sum(before, axis=1, keepdims=True)
    eye = iota((LANE, LANE), 0) == iota((LANE, LANE), 1)
    carry = jnp.sum(jnp.where(eye, before, 0.0), axis=0, keepdims=True)
    first_row = iota((chunk, LANE), 0) == 0

    def col_copy(d, m):
        to = (col + d) % ncol
        return pltpu.make_async_remote_copy(
            src_ref=outgoing.at[m, to],
            dst_ref=incoming.at[m, d - 1],
            send_sem=col_send.at[m, d - 1],
            recv_sem=col_recv.at[m, d - 1],
            device_id=(row, to),
            device_id_type=MESH,
        )

    def bin_chunk(i, carry):
        m = (row + 1 + i) % nrow
        if not early:
            build(m, 0)
        slot = m if early else 0
        product = lax.dot_general(
            onehot[slot], windows[...], (((1,), (1,)), ((), ())), preferred_element_type=f32
        )
        tail = product[:, LANE:]
        shifted = jnp.where(first_row, carry, pltpu.roll(tail, 1, 0))
        cells = product[:, :LANE] + shifted
        outgoing[m] = cells.astype(bf16).reshape(ncol, TILES_DEV, LANE)
        for d in range(1, ncol):
            col_copy(d, m).start()
        return tail[chunk - 1 :, :]

    lax.fori_loop(0, nrow, bin_chunk, carry)

    def add_chunk(m):
        value = outgoing[m, col].astype(f32)
        for d in range(1, ncol):
            col_copy(d, m).wait_recv()
            value = value + incoming[m, d - 1].astype(f32)
        return value

    row_copies = []
    for d in range(1, nrow):
        to = (row + d) % nrow
        totals[d - 1] = add_chunk(to)
        copy = pltpu.make_async_remote_copy(
            src_ref=totals.at[d - 1],
            dst_ref=arrived.at[d - 1],
            send_sem=row_send.at[d - 1],
            recv_sem=row_recv.at[d - 1],
            device_id=(to, col),
            device_id_type=MESH,
        )
        copy.start()
        row_copies.append(copy)
    value = add_chunk(row)
    for d in range(1, nrow):
        row_copies[d - 1].wait_recv()
        value = value + arrived[d - 1]
    spec_ref[...] = value

    for copy in started + amp_copies + row_copies:
        copy.wait_send()

    def drain(m, _):
        for d in range(1, ncol):
            col_copy(d, m).wait_send()
        return 0

    lax.fori_loop(0, nrow, drain, 0)
    pl.when(row < nrow - 1)(lambda: up.wait_send())
    pl.when(row > 0)(lambda: down.wait_send())


def shards(
    lower_vectors,
    upper_vectors,
    vib_dipole,
    rot_factor,
    population,
    broadening,
    lower_symmetry,
    upper_symmetry,
    symmetry_pairs,
    width_class,
    width_table,
    line_shard,
    line_bin,
    bin_offset,
):
    nrow, ncol = lax.axis_size("row"), lax.axis_size("col")
    lows, basis = lower_vectors.shape
    uppers = upper_vectors.shape[0]
    low_rows, lines = line_bin.shape
    quarter = basis // 4
    cuts = [lower_vectors[:, i * quarter : (i + 1) * quarter] for i in (0, 2, 1, 3)]
    pieces = jnp.concatenate(cuts, axis=0).reshape(2, 2 * lows, quarter)
    chunk = ncol * TILES_DEV
    count = low_rows * lines
    early = nrow * chunk * count * 2 <= 26 * 2**20
    vmem = pl.BlockSpec(memory_space=pltpu.VMEM)
    smem = pl.BlockSpec(memory_space=pltpu.SMEM)
    hbm = pl.BlockSpec(memory_space=pl.ANY)
    dma = pltpu.SemaphoreType.DMA
    amplitudes, spectrum = pl.pallas_call(
        functools.partial(kernel, nrow, ncol),
        out_shape=(
            jax.ShapeDtypeStruct((low_rows, lines), f32),
            jax.ShapeDtypeStruct((TILES_DEV, LANE), f32),
        ),
        in_specs=[hbm, hbm, vmem, smem, vmem, vmem, vmem, vmem, smem, vmem, smem, vmem, vmem, vmem],
        out_specs=(vmem, vmem),
        scratch_shapes=[
            pltpu.VMEM((uppers, basis + 2 * NV), bf16),
            pltpu.VMEM((2 * uppers, basis // 2), bf16),
            pltpu.VMEM((2, ncol * 2 * lows, quarter), bf16),
            pltpu.VMEM((ncol * lows, uppers), f32),
            pltpu.VMEM((nrow - 1, low_rows, lines), f32),
            pltpu.VMEM((6, low_rows, lines), f32),
            pltpu.VMEM((2, low_rows, lines), jnp.int32),
            pltpu.VMEM((low_rows, LANE, lines), f32),
            pltpu.VMEM((2 * LANE, count), bf16),
            pltpu.VMEM((nrow if early else 1, chunk, count), bf16),
            pltpu.VMEM((nrow, ncol, TILES_DEV, LANE), bf16),
            pltpu.VMEM((nrow, ncol - 1, TILES_DEV, LANE), bf16),
            pltpu.VMEM((nrow - 1, TILES_DEV, LANE), f32),
            pltpu.VMEM((nrow - 1, TILES_DEV, LANE), f32),
            dma((2,)),
            dma((2,)),
            dma((2,)),
            dma((2, ncol)),
            dma((2, ncol)),
            dma((2, nrow - 1)),
            dma((2, nrow - 1)),
            dma((nrow, ncol - 1)),
            dma((nrow, ncol - 1)),
            dma((nrow - 1,)),
            dma((nrow - 1,)),
        ],
        compiler_params=pltpu.CompilerParams(
            collective_id=0, has_side_effects=True, vmem_limit_bytes=58 * 2**20
        ),
    )(
        pieces,
        upper_vectors,
        vib_dipole,
        rot_factor,
        population[None, :],
        broadening[None, :],
        lower_symmetry[None, :],
        upper_symmetry[None, :],
        symmetry_pairs,
        width_class,
        width_table,
        line_shard,
        line_bin,
        bin_offset,
    )
    return (amplitudes, spectrum.reshape(GRID_DEV))


def solution(mesh):
    return jax.shard_map(
        shards,
        mesh=mesh,
        in_specs=(
            P("col", "row"),
            P("col", "row"),
            P(),
            P(None, "row"),
            P("row"),
            P("row"),
            P("row"),
            P("col"),
            P(),
            P("row", "col"),
            P(),
            P("row", "col"),
            P("row", "col"),
            P("row", "col"),
        ),
        out_specs=(P("row", "col"), P(("row", "col"))),
        check_vma=False,
    )
```

```python
import functools
import math

import jax
import jax.numpy as jnp
from jax import lax
from jax.experimental import pallas as pl
from jax.experimental.pallas import tpu as pltpu
from jax.sharding import PartitionSpec as P

NV = 256
HW = 64
GRID_DEV = 8192
LANE = 128
TILES_DEV = GRID_DEV // LANE
GROUP = 4
PIECES = 4
MESH = pl.DeviceIdType.MESH

doppler_base = 1.5
log_two = math.log(2.0)

f32 = jnp.float32
bf16 = jnp.bfloat16


def flip(index, mask):
    bit = 1
    while bit <= mask:
        if mask & bit:
            index = index + bit - 2 * bit * ((index // bit) % 2)
        bit *= 2
    return index


def iota(shape, dim):
    return lax.broadcasted_iota(jnp.int32, shape, dim)


def column_of(row_value):
    n = row_value.shape[1]
    eye = iota((n, n), 0) == iota((n, n), 1)
    return jnp.sum(jnp.where(eye, row_value, jnp.zeros_like(row_value)), axis=1, keepdims=True)


def kernel(
    nrow,
    ncol,
    lower_ref,
    upper_ref,
    vib_ref,
    rot_ref,
    population_ref,
    broadening_ref,
    lower_sym_ref,
    upper_sym_ref,
    pairs_ref,
    width_class_ref,
    table_ref,
    shard_ref,
    bin_ref,
    offset_ref,
    amp_ref,
    spec_ref,
    padded,
    weighted,
    gathered,
    partial,
    amp_in,
    coef,
    place,
    unit,
    windows,
    onehot,
    outgoing,
    incoming,
    totals,
    arrived,
    local_sem,
    halo_send,
    halo_recv,
    gather_send,
    gather_recv,
    amp_send,
    amp_recv,
    col_send,
    col_recv,
    row_send,
    row_recv,
):
    row = lax.axis_index("row")
    col = lax.axis_index("col")
    uppers, basis = upper_ref.shape
    slabs = basis // NV
    lows = lower_ref.shape[0]
    pieces, _, piece = gathered.shape
    pair_rows = 2 * lows
    low_rows, lines = bin_ref.shape
    tiles = nrow * ncol * TILES_DEV
    chunk = ncol * TILES_DEV
    bits = []
    bit = ncol // 2
    while bit:
        bits.append(bit)
        bit //= 2
    both = [bits, [bits[1], bits[0]] + bits[2:]]
    orders = [both[k % 2] for k in range(pieces)]

    load = pltpu.make_async_copy(upper_ref, padded.at[:, pl.ds(NV, basis)], local_sem.at[0])
    load.start()

    barrier = pltpu.get_barrier_semaphore()
    for d in range(1, ncol):
        pl.semaphore_signal(
            barrier, inc=1, device_id=(row, (col + d) % ncol), device_id_type=MESH
        )
    for d in range(1, nrow):
        pl.semaphore_signal(
            barrier, inc=1, device_id=((row + d) % nrow, col), device_id_type=MESH
        )
    for k in range(pieces):
        sides = [lower_ref[:, pl.ds(i * (basis // 2) + k * piece, piece)] for i in range(2)]
        gathered[k, pl.ds(0, pair_rows), :] = jnp.concatenate(sides, axis=0)
    pl.semaphore_wait(barrier, ncol + nrow - 2)

    def slot_rows(mask):
        at = mask // 2 + (mask % 2) * (ncol // 2)
        return pl.ds(at * pair_rows, pair_rows)

    def piece_copy(half, mask, bit):
        to = mask ^ bit
        return pltpu.make_async_remote_copy(
            src_ref=gathered.at[half, slot_rows(mask)],
            dst_ref=gathered.at[half, slot_rows(to)],
            send_sem=gather_send.at[half, to],
            recv_sem=gather_recv.at[half, to],
            device_id=(row, flip(col, bit)),
            device_id_type=MESH,
        )

    up = pltpu.make_async_remote_copy(
        src_ref=upper_ref.at[:, pl.ds(basis - NV, NV)],
        dst_ref=padded.at[:, pl.ds(0, NV)],
        send_sem=halo_send.at[0],
        recv_sem=halo_recv.at[0],
        device_id=((row + 1) % nrow, col),
        device_id_type=MESH,
    )
    down = pltpu.make_async_remote_copy(
        src_ref=upper_ref.at[:, pl.ds(0, NV)],
        dst_ref=padded.at[:, pl.ds(basis + NV, NV)],
        send_sem=halo_send.at[1],
        recv_sem=halo_recv.at[1],
        device_id=((row + nrow - 1) % nrow, col),
        device_id_type=MESH,
    )
    pl.when(row < nrow - 1)(lambda: up.start())
    pl.when(row > 0)(lambda: down.start())

    started = []

    def send(half, mask, bit):
        copy = piece_copy(half, mask, bit)
        copy.start()
        started.append(copy)

    for level in range(len(bits)):
        for half in range(pieces):
            send(half, 0, orders[half][level])

    broad = column_of(broadening_ref[...])
    width_class = width_class_ref[...]
    lorentz = jnp.zeros(width_class.shape, f32)
    for i in range(table_ref.shape[0]):
        lorentz = lorentz + jnp.where(width_class == i, table_ref[i], 0.0)
    lorentz = lorentz * broad
    position = shard_ref[...] * GRID_DEV + bin_ref[...]
    center = position.astype(f32) + offset_ref[...]
    doppler = doppler_base * (1.0 + center / float(GRID_DEV * nrow * ncol))
    mixing = lorentz / (lorentz + doppler)
    coef[0] = mixing * lorentz / math.pi
    coef[1] = lorentz * lorentz
    coef[2] = (1.0 - mixing) * (math.sqrt(log_two / math.pi) / doppler)
    coef[3] = -log_two / (doppler * doppler)
    coef[4] = offset_ref[...]
    start = position - HW
    place[0] = lax.shift_right_arithmetic(start, 7)
    place[1] = lax.bitwise_and(start, LANE - 1)

    cell = iota((LANE, lines), 0)

    def shape_row(r, _):
        inside = place[1, pl.ds(r, 1), :]
        step = lax.bitwise_and(cell - inside, LANE - 1) - HW
        x = step.astype(f32) - coef[4, pl.ds(r, 1), :]
        square = x * x
        unit[r] = coef[0, pl.ds(r, 1), :] / (square + coef[1, pl.ds(r, 1), :]) + coef[
            2, pl.ds(r, 1), :
        ] * jnp.exp(coef[3, pl.ds(r, 1), :] * square)
        return 0

    lax.fori_loop(0, low_rows, shape_row, 0)

    tile_iota = iota((chunk, lines), 0)

    def build(m, slot):
        def build_row(r, _):
            tile = place[0, pl.ds(r, 1), :]
            tile = jnp.where(tile < 0, tile + tiles, tile) - m * chunk
            hit = jnp.where(tile_iota == tile, 1.0, 0.0).astype(bf16)
            onehot[slot, :, pl.ds(pl.multiple_of(r * lines, lines), lines)] = hit
            return 0

        lax.fori_loop(0, low_rows, build_row, 0)

    early = onehot.shape[0] == nrow
    if early:
        lax.fori_loop(0, nrow, lambda m, _: (build(m, m), 0)[1], 0)

    load.wait()

    @pl.when(row == 0)
    def _():
        padded[:, pl.ds(0, NV)] = jnp.zeros((uppers, NV), bf16)

    @pl.when(row == nrow - 1)
    def _():
        padded[:, pl.ds(basis + NV, NV)] = jnp.zeros((uppers, NV), bf16)

    half_slabs = slabs // 2

    def weigh(g, _):
        first = g * GROUP
        sums = [jnp.zeros((uppers, NV), f32) for _ in range(GROUP)]
        for band in range(3):
            blocks = [
                padded[:, pl.ds(pl.multiple_of((first + j + band) * NV, NV), NV)]
                for j in range(GROUP)
            ]
            product = lax.dot_general(
                jnp.concatenate(blocks, axis=0),
                vib_ref[band],
                (((1,), (1,)), ((), ())),
                preferred_element_type=f32,
            )
            for j in range(GROUP):
                sums[j] = sums[j] + rot_ref[band, first + j] * product[j * uppers : (j + 1) * uppers]
        part = first // half_slabs
        for j in range(GROUP):
            at = pl.multiple_of((first + j - part * half_slabs) * NV, NV)
            weighted[pl.ds(pl.multiple_of(part * uppers, uppers), uppers), pl.ds(at, NV)] = sums[
                j
            ].astype(bf16)
        return 0

    def weigh_half(part):
        steps = half_slabs // GROUP
        lax.fori_loop(part * steps, (part + 1) * steps, weigh, 0)

    pl.when(row > 0)(lambda: up.wait_recv())
    weigh_half(0)

    def slots_of(half, level):
        order = orders[half]
        masks = [0]
        for b in order[:level]:
            masks = masks + [m ^ b for m in masks]
        return [(m, m ^ order[level]) for m in masks]

    def forward(level, begin=0, end=None, halves=range(pieces)):
        count = len(slots_of(0, level))
        for i in range(begin, count if end is None else end):
            for half in halves:
                mask, slot = slots_of(half, level)[i]
                piece_copy(half, mask, orders[half][level]).wait_recv()
                for later in orders[half][level + 1 :]:
                    send(half, slot, later)

    forward(0)
    forward(1, 0, 1)
    pl.when(row < nrow - 1)(lambda: down.wait_recv())

    weigh_half(1)

    last = len(bits) - 1
    total = jnp.zeros((ncol * pair_rows, 2 * uppers), f32)
    for step in range(pieces + 2):
        if step < pieces:
            if last > 1:
                forward(1, 1, None, [step])
            for level in range(2, last):
                forward(level, 0, None, [step])
        if step >= 2:
            k = step - 2
            forward(last, 0 if last > 1 else 1, None, [k])
            total = total + lax.dot_general(
                gathered[k],
                weighted[:, pl.ds(k * piece, piece)],
                (((1,), (1,)), ((), ())),
                preferred_element_type=f32,
            )
    for i in range(ncol):
        base = i * pair_rows
        rows = total[base : base + lows, :uppers] + total[base + lows : base + 2 * lows, uppers:]
        source = flip(col, 2 * (i % (ncol // 2)) + i // (ncol // 2))
        partial[pl.ds(pl.multiple_of(source * lows, 8), lows), :] = rows
    amp_copies = []
    for d in range(1, nrow):
        to = (row + d) % nrow
        copy = pltpu.make_async_remote_copy(
            src_ref=partial.at[pl.ds(pl.multiple_of(to * low_rows, 8), low_rows)],
            dst_ref=amp_in.at[d - 1],
            send_sem=amp_send.at[d - 1],
            recv_sem=amp_recv.at[d - 1],
            device_id=(to, col),
            device_id_type=MESH,
        )
        copy.start()
        amp_copies.append(copy)
    population = column_of(population_ref[...])
    lower_sym = lower_sym_ref[...]
    allowed = jnp.zeros(lower_sym.shape, jnp.int32)
    for i in range(pairs_ref.shape[0]):
        allowed = allowed + jnp.where(lower_sym == i, pairs_ref[i], 0)
    allowed = column_of(allowed)
    keep = jnp.where(upper_sym_ref[...] == allowed, 1.0, 0.0)
    amplitudes = partial[pl.ds(pl.multiple_of(row * low_rows, 8), low_rows), :]
    for copy in amp_copies:
        copy.wait_recv()
    for d in range(1, nrow):
        amplitudes = amplitudes + amp_in[d - 1]
    amp_ref[...] = amplitudes
    coef[5] = population * amplitudes * amplitudes * keep

    first_tile = ((row + 1) % nrow) * chunk

    def scale_row(r, before):
        inside = place[1, pl.ds(r, 1), :]
        tile = place[0, pl.ds(r, 1), :]
        value = unit[r] * coef[5, pl.ds(r, 1), :]
        is_head = cell >= inside
        head = jnp.where(is_head & (tile >= 0), value, 0.0)
        tail = jnp.where(is_head | (tile >= tiles - 1), 0.0, value)
        lane = pl.ds(pl.multiple_of(r * lines, lines), lines)
        windows[pl.ds(0, LANE), lane] = head.astype(bf16)
        windows[pl.ds(LANE, LANE), lane] = tail.astype(bf16)
        return before + jnp.where(tile == first_tile - 1, tail, 0.0)

    before = lax.fori_loop(0, low_rows, scale_row, jnp.zeros((LANE, lines), f32))
    before = jnp.sum(before, axis=1, keepdims=True)
    eye = iota((LANE, LANE), 0) == iota((LANE, LANE), 1)
    carry = jnp.sum(jnp.where(eye, before, 0.0), axis=0, keepdims=True)
    first_row = iota((chunk, LANE), 0) == 0

    def col_copy(d, m):
        to = (col + d) % ncol
        return pltpu.make_async_remote_copy(
            src_ref=outgoing.at[m, to],
            dst_ref=incoming.at[m, d - 1],
            send_sem=col_send.at[m, d - 1],
            recv_sem=col_recv.at[m, d - 1],
            device_id=(row, to),
            device_id_type=MESH,
        )

    def bin_chunk(i, carry):
        m = (row + 1 + i) % nrow
        if not early:
            build(m, 0)
        slot = m if early else 0
        product = lax.dot_general(
            onehot[slot], windows[...], (((1,), (1,)), ((), ())), preferred_element_type=f32
        )
        tail = product[:, LANE:]
        shifted = jnp.where(first_row, carry, pltpu.roll(tail, 1, 0))
        cells = product[:, :LANE] + shifted
        outgoing[m] = cells.astype(bf16).reshape(ncol, TILES_DEV, LANE)
        for d in range(1, ncol):
            col_copy(d, m).start()
        return tail[chunk - 1 :, :]

    lax.fori_loop(0, nrow, bin_chunk, carry)

    def add_chunk(m):
        value = outgoing[m, col].astype(f32)
        for d in range(1, ncol):
            col_copy(d, m).wait_recv()
            value = value + incoming[m, d - 1].astype(f32)
        return value

    row_copies = []
    for d in range(1, nrow):
        to = (row + d) % nrow
        totals[d - 1] = add_chunk(to)
        copy = pltpu.make_async_remote_copy(
            src_ref=totals.at[d - 1],
            dst_ref=arrived.at[d - 1],
            send_sem=row_send.at[d - 1],
            recv_sem=row_recv.at[d - 1],
            device_id=(to, col),
            device_id_type=MESH,
        )
        copy.start()
        row_copies.append(copy)
    value = add_chunk(row)
    for d in range(1, nrow):
        row_copies[d - 1].wait_recv()
        value = value + arrived[d - 1]
    spec_ref[...] = value

    for copy in started + amp_copies + row_copies:
        copy.wait_send()

    def drain(m, _):
        for d in range(1, ncol):
            col_copy(d, m).wait_send()
        return 0

    lax.fori_loop(0, nrow, drain, 0)
    pl.when(row < nrow - 1)(lambda: up.wait_send())
    pl.when(row > 0)(lambda: down.wait_send())


def hand_over(amp_ref, spec_ref, amp_out, spec_out):
    amp_out[...] = amp_ref[...]
    spec_out[...] = spec_ref[...]


def shards(
    lower_vectors,
    upper_vectors,
    vib_dipole,
    rot_factor,
    population,
    broadening,
    lower_symmetry,
    upper_symmetry,
    symmetry_pairs,
    width_class,
    width_table,
    line_shard,
    line_bin,
    bin_offset,
):
    nrow, ncol = lax.axis_size("row"), lax.axis_size("col")
    lows, basis = lower_vectors.shape
    uppers = upper_vectors.shape[0]
    low_rows, lines = line_bin.shape
    piece = basis // 2 // PIECES
    chunk = ncol * TILES_DEV
    count = low_rows * lines
    early = nrow * chunk * count * 2 <= 26 * 2**20
    vmem = pl.BlockSpec(memory_space=pltpu.VMEM)
    smem = pl.BlockSpec(memory_space=pltpu.SMEM)
    hbm = pl.BlockSpec(memory_space=pl.ANY)
    dma = pltpu.SemaphoreType.DMA
    amplitudes, spectrum = pl.pallas_call(
        functools.partial(kernel, nrow, ncol),
        out_shape=(
            jax.ShapeDtypeStruct((low_rows, lines), f32),
            jax.ShapeDtypeStruct((TILES_DEV, LANE), f32),
        ),
        in_specs=[vmem, hbm, vmem, smem, vmem, vmem, vmem, vmem, smem, vmem, smem, vmem, vmem, vmem],
        out_specs=(vmem, vmem),
        scratch_shapes=[
            pltpu.VMEM((uppers, basis + 2 * NV), bf16),
            pltpu.VMEM((2 * uppers, basis // 2), bf16),
            pltpu.VMEM((PIECES, ncol * 2 * lows, piece), bf16),
            pltpu.VMEM((ncol * lows, uppers), f32),
            pltpu.VMEM((nrow - 1, low_rows, lines), f32),
            pltpu.VMEM((6, low_rows, lines), f32),
            pltpu.VMEM((2, low_rows, lines), jnp.int32),
            pltpu.VMEM((low_rows, LANE, lines), f32),
            pltpu.VMEM((2 * LANE, count), bf16),
            pltpu.VMEM((nrow if early else 1, chunk, count), bf16),
            pltpu.VMEM((nrow, ncol, TILES_DEV, LANE), bf16),
            pltpu.VMEM((nrow, ncol - 1, TILES_DEV, LANE), bf16),
            pltpu.VMEM((nrow - 1, TILES_DEV, LANE), f32),
            pltpu.VMEM((nrow - 1, TILES_DEV, LANE), f32),
            dma((1,)),
            dma((2,)),
            dma((2,)),
            dma((PIECES, ncol)),
            dma((PIECES, ncol)),
            dma((nrow - 1,)),
            dma((nrow - 1,)),
            dma((nrow, ncol - 1)),
            dma((nrow, ncol - 1)),
            dma((nrow - 1,)),
            dma((nrow - 1,)),
        ],
        compiler_params=pltpu.CompilerParams(
            collective_id=0, has_side_effects=True, vmem_limit_bytes=58 * 2**20
        ),
    )(
        lower_vectors,
        upper_vectors,
        vib_dipole,
        rot_factor,
        population[None, :],
        broadening[None, :],
        lower_symmetry[None, :],
        upper_symmetry[None, :],
        symmetry_pairs,
        width_class,
        width_table,
        line_shard,
        line_bin,
        bin_offset,
    )
    amplitudes, spectrum = pl.pallas_call(
        hand_over,
        out_shape=(
            jax.ShapeDtypeStruct((low_rows, lines), f32),
            jax.ShapeDtypeStruct((TILES_DEV, LANE), f32),
        ),
        in_specs=[vmem, vmem],
        out_specs=(vmem, vmem),
    )(amplitudes, spectrum)
    return (amplitudes, spectrum.reshape(GRID_DEV))


def solution(mesh):
    return jax.shard_map(
        shards,
        mesh=mesh,
        in_specs=(
            P("col", "row"),
            P("col", "row"),
            P(),
            P(None, "row"),
            P("row"),
            P("row"),
            P("row"),
            P("col"),
            P(),
            P("row", "col"),
            P(),
            P("row", "col"),
            P("row", "col"),
            P("row", "col"),
        ),
        out_specs=(P("row", "col"), P(("row", "col"))),
        check_vma=False,
    )
```
